256 devices in a mesh: ctx: 8 (over z_hi, core), ex: 32 (over y, z_lo, x).
Axes of the slice: x: 4, y: 4, z: 8 (z_hi: 4, z_lo: 2; z = z_hi * 2 + z_lo), core: 2. Of those that a mesh axis runs over, the one named last changes fastest.
Arguments:
- acts: bfloat16 [32, 1024, 8192], P('ex', 'ctx'), may hold values from -6 to 6
- out_grads: bfloat16 [32, 1024, 8192], P('ex', 'ctx'), may hold values from -6 to 6
- projections: bfloat16 [2, 8192, 256], P(None, 'ex', 'ctx'), may hold values from -0.0625 to 0.0625
- segments: int32 [32, 1024], P('ex', 'ctx'), may hold values from 0 to 3, never falling along the last dimension, each value on 1 to 512 neighbouring positions
- valid: int32 [32, 1024], P('ex', 'ctx'), may hold values 0 or 1
- stored: bfloat16 [98304, 8192], P('ex', 'ctx'), may hold values from -60 to 60, as said below
Outputs:
- scores: float32 [128, 98304], P('ctx', 'ex')
The draws below stay inside these ranges and needn't reach their ends.
Inputs may be any that keep to these rules, and one draw needn't show every extreme that they name: `stored`: finite real values.
All inputs are finite; a program needn't handle non-finite values. No bound on the sum of `valid` on one device may be relied on, other than what follows from the above.
Results may differ from the reference program's by a relative error of at most 0.005.
Values may be sent and summed in bfloat16 or wider, within the bound.
A program may use at most 128 MiB of HBM per device.

```python
import math
import jax
import jax.numpy as jnp
import numpy as np
from jax import lax

D = 8192
RANK = 32
MODULES = 8
FEAT = 1024
DOCS = 4
STEPS = 4
LEN = 1024
STORE = 98304
N_EX = 32


def draw_stored(key, part):
    key = jax.random.fold_in(key, 11)
    key_entries, key_rough = jax.random.split(key)
    positions = jnp.arange(STORE).astype(jnp.float32)
    rising = jnp.exp(math.log(3.0) * positions / (STORE - 1))
    entries = jax.random.truncated_normal(key_entries, -4.0, 4.0, (STORE, MODULES * FEAT), jnp.float32)
    rough = jnp.exp(jax.random.uniform(key_rough, (STORE,), jnp.float32, -0.35, 0.35))
    return (entries * (rising * rough)[:, None]).astype(jnp.bfloat16)


def set_ends(array, own_key, low, largest):
    index_at = [jax.random.randint(jax.random.fold_in(own_key, axis), (), 0, length) for axis, length in enumerate(array.shape)]
    widest = array.shape.index(max(array.shape))
    beside = index_at[:widest] + [(index_at[widest] + 1) % array.shape[widest]] + index_at[widest + 1:]
    return array.at[tuple(index_at)].set(low).at[tuple(beside)].set(largest)


def level_of(own_key, dims, cuts, least, top_value):
    def one(dim, blocks):
        steps = jax.random.uniform(jax.random.fold_in(jax.random.fold_in(own_key, 6), dim), (blocks,), jnp.float32, least / len(cuts), top_value / len(cuts))
        return jnp.repeat(jnp.exp(steps), dims[dim] // blocks).reshape((-1,) + (1,) * (len(dims) - dim - 1))

    gain = one(*cuts[0])
    for cut in cuts[1:]:
        gain = gain * one(*cut)
    return gain


def split_up(number_of, total, bound, slope):
    loads = [(1 << 20) // math.isqrt(rank ** slope) + 1 for rank in range(2, number_of + 1)]
    surplus, given = total - bound - (number_of - 1), [1] * (number_of - 1)
    while surplus > 0:
        free = [i for i in range(number_of - 1) if given[i] < bound]
        whole, left = sum([loads[i] for i in free]), surplus
        for i in free:
            addition = min(bound - given[i], max(1, left * loads[i] // whole), surplus)
            given[i] = given[i] + addition
            surplus = surplus - addition
    return np.array([bound] + given)


def ragged_sizes(rng, amount, total, most, skew):
    if amount == 2:
        one = jax.random.randint(rng, (), max(1, total - most), min(most, total - 1) + 1)
        return jnp.stack([one, total - one])
    sizes = jnp.asarray(split_up(amount, total, most, skew), jnp.int32)
    pairs = (amount - 1) // 2
    source_of, sink = sizes[1:1 + 2 * pairs:2], sizes[2:2 + 2 * pairs:2]
    margin = jnp.minimum(source_of - 1, most - sink)
    shifted = jax.random.randint(jax.random.fold_in(rng, 1), (pairs,), 0, 1 << 20) % (margin + 1)
    sizes = sizes.at[1:1 + 2 * pairs:2].set(source_of - shifted).at[2:2 + 2 * pairs:2].set(sink + shifted)
    return sizes[jax.random.permutation(jax.random.fold_in(rng, 2), amount)]


def noise(rng, shape, scale, bound, shards=(), kind=jnp.bfloat16):
    drawn = jax.random.normal(rng, shape, jnp.float32) * scale
    if len(shards) > 0:
        drawn = level_of(rng, shape, shards, -0.22, 0.18) * drawn
    return jnp.clip(drawn, min=-bound, max=bound).astype(kind)


def setup_inputs(seed: int = 0) -> dict:
    seeds = jax.random.split(jax.random.key(seed), 7)
    return {
        "acts": noise(seeds[0], (N_EX, LEN, D), 1.0, 6.0, ((0, 32), (1, 8))),
        "out_grads": noise(seeds[1], (N_EX, LEN, D), 1.0, 6.0, ((0, 32), (1, 8))),
        "projections": noise(seeds[2], (2, D, MODULES * RANK), D ** -0.5, 0.0625, ((1, 32), (2, 8))),
        "segments": jax.vmap(lambda own: jnp.searchsorted(jnp.cumsum(ragged_sizes(own, DOCS, LEN, LEN // 2, 1)), jnp.arange(LEN), side="right"))(jax.random.split(seeds[3], N_EX)).reshape((N_EX, LEN)).astype(jnp.int32),
        "valid": set_ends((jax.random.randint(seeds[4], (N_EX, LEN), 0, 8) < 7).astype(jnp.int32), jax.random.fold_in(seeds[4], 1), 0, 1),
        "stored": draw_stored(jax.random.fold_in(seeds[6], 71), 0),
    }


damping = 0.1
spread = 1.5
epsilon = 1e-06

def reference(acts, out_grads, projections, segments, valid, stored):
    doc_ids = jnp.arange(DOCS, dtype=jnp.int32)

    def one_context(packed):
        x_rows, g_rows, seg_rows, ok_rows = packed
        x_proj = jnp.dot(x_rows, projections[0], preferred_element_type=jnp.float32).astype(jnp.bfloat16)
        g_proj = jnp.dot(g_rows, projections[1], preferred_element_type=jnp.float32).astype(jnp.bfloat16)
        onehot = ((seg_rows[None, :] == doc_ids[:, None]) & (ok_rows[None, :] == 1)).astype(jnp.bfloat16)
        weighted = (onehot[:, :, None] * g_proj[None, :, :]).reshape(DOCS, LEN, MODULES, RANK)
        summed = jnp.einsum('qtmi,tmj->qmij', weighted.astype(jnp.float32), x_proj.reshape(LEN, MODULES, RANK).astype(jnp.float32))
        return summed.reshape(DOCS, MODULES, FEAT)
    queries = lax.map(one_context, (acts, out_grads, segments, valid)).reshape(N_EX * DOCS, MODULES, FEAT)

    def module_gram(module):
        columns = lax.dynamic_slice_in_dim(stored, module * FEAT, FEAT, 1)
        return jnp.dot(columns.T, columns, preferred_element_type=jnp.float32) / STORE
    curvature = lax.map(module_gram, jnp.arange(MODULES, dtype=jnp.int32))
    mean_diag = jnp.trace(curvature, axis1=1, axis2=2) / FEAT
    step_size = (1.0 / (spread * (mean_diag + epsilon)))[None, :, None]

    def apply_fisher(iterate):
        return jnp.einsum('mfg,qmg->qmf', curvature, iterate, precision=lax.Precision.HIGHEST) + damping * mean_diag[None, :, None] * iterate
    iterate = step_size * queries
    for iteration in range(STEPS):
        iterate = iterate + step_size * (queries - apply_fisher(iterate))
    precond = iterate.astype(jnp.bfloat16).reshape(N_EX * DOCS, MODULES * FEAT)
    score_scale = 1.0 / math.sqrt(MODULES * FEAT * LEN / DOCS)
    raw_scores = lax.dot_general(precond, stored, (((1,), (1,)), ((), ())), preferred_element_type=jnp.float32)
    return raw_scores * score_scale
```

```python
import math

import jax
import jax.numpy as jnp
from jax import lax
from jax.experimental import pallas as pl
from jax.experimental.pallas import tpu as pltpu
from jax.sharding import PartitionSpec as P

RANK = 32
MODULES = 8
DOCS = 4
STEPS = 4
FEAT = 1024
STORE = 98304
LEN = 1024

damping = 0.1
spread = 1.5
epsilon = 1e-06

MESH = pl.DeviceIdType.MESH
F32 = jnp.float32
BF16 = jnp.bfloat16

N_EX = 32
CHUNKS = 4
BLK = 256
NBLK = FEAT // BLK
PAIRS = [(i, j) for i in range(NBLK) for j in range(i, NBLK)]
PIECE = len(PAIRS) * BLK // N_EX

NN = (((1,), (0,)), ((), ()))
NT = (((1,), (1,)), ((), ()))
TN = (((0,), (0,)), ((), ()))


def dot(a, b, dims):
    return lax.dot_general(a, b, dims, preferred_element_type=F32)


def kernel(
    pt, acts, grads, seg, val, stored, out,
    wa, wb, xa, ga, sv, wm, gsend, grecv, cb, tsend, trecv, qs, qg, part, sib, zsend, zrecv,
    loc_sem, sib_s, sib_r, z_s, z_r, ring_s, ring_r, g_s, g_r, c_s, c_r, t_s, t_r, q_s, q_r,
    o_s, o_r, zo_s, zo_r,
):
    ctx = lax.axis_index("ctx")
    ex = lax.axis_index("ex")
    zh, core = ctx // 2, ctx % 2
    y, zl, x = ex // 8, (ex // 4) % 2, ex % 4
    z = zh * 2 + zl

    def at(xx, yy, zz):
        return {"ctx": (zz // 2) * 2 + core, "ex": (yy * 2 + zz % 2) * 4 + xx}

    sibling = {"ctx": zh * 2 + 1 - core, "ex": ex}

    def remote(src, dst, s, r, device):
        return pltpu.make_async_remote_copy(
            src_ref=src, dst_ref=dst, send_sem=s, recv_sem=r, device_id=device, device_id_type=MESH
        )

    load_s = pltpu.make_async_copy(stored, sv, loc_sem.at[0])
    load_x = pltpu.make_async_copy(acts.at[0], xa.at[0], loc_sem.at[1])
    load_g = pltpu.make_async_copy(grads.at[0], ga.at[0], loc_sem.at[2])
    load_s.start()
    load_x.start()
    load_g.start()

    barrier = pltpu.get_barrier_semaphore()

    def greet(k, carry):
        pl.semaphore_signal(
            barrier, inc=1, device_id={"ctx": ctx, "ex": (ex + k) % N_EX}, device_id_type=MESH
        )
        return carry

    lax.fori_loop(1, N_EX, greet, 0)
    for dh in range(1, 4):
        for l in range(2):
            pl.semaphore_signal(
                barrier, inc=1, device_id=at(x, y, ((zh + dh) % 4) * 2 + l), device_id_type=MESH
            )
    pl.semaphore_signal(barrier, inc=1, device_id=sibling, device_id_type=MESH)
    for d in range(8):
        wm[0, d : d + 1, :] = jnp.where((seg[...] == d) & (val[...] == 1), 1.0, 0.0).astype(F32)
    wa[x, y, zl, zh] = pt[0]
    wb[y, x, zl, zh] = pt[1]
    pl.semaphore_wait(barrier, N_EX - 1 + 7)

    swaps = [
        remote(acts.at[0], xa.at[1], sib_s.at[0], sib_r.at[0], sibling),
        remote(grads.at[0], ga.at[1], sib_s.at[1], sib_r.at[1], sibling),
        remote(wm.at[0], wm.at[1], sib_s.at[2], sib_r.at[2], sibling),
    ]

    def along_z(d, a):
        slot = wa.at[x, y, zl, zh] if a == 0 else wb.at[y, x, zl, zh]
        return remote(pt.at[a], slot, z_s.at[a, d], z_r.at[a, d], at(x, y, (z + d) % 8))

    def z_arrival(d, a):
        zz = (z + 8 - d) % 8
        slot = wa.at[x, y, zz % 2, zz // 2] if a == 0 else wb.at[y, x, zz % 2, zz // 2]
        return remote(pt.at[a], slot, z_s.at[a, d], z_r.at[a, d], at(x, y, zz))

    for d in (1, 7, 2, 6, 3, 5, 4):
        for a in range(2):
            along_z(d, a).start()
    for copy in swaps:
        copy.start()

    xp_, xm, xo = (x + 1) % 4, (x + 3) % 4, (x + 2) % 4
    yp_, ym, yo = (y + 1) % 4, (y + 3) % 4, (y + 2) % 4

    def ring_pairs(block, half, where, me, plus, minus, opposite, first):
        def one(ref, k, device):
            return remote(ref, ref, ring_s.at[first + k], ring_r.at[first + k], device)

        own = [one(block(me), 0, where(plus)), one(block(me), 1, where(minus))]
        onward = [one(half(minus, 0), 2, where(plus)), one(half(plus, 1), 3, where(minus))]
        own_in = [one(block(minus), 0, where(minus)), one(block(plus), 1, where(plus))]
        onward_in = [one(half(opposite, 0), 2, where(minus)), one(half(opposite, 1), 3, where(plus))]
        return own, onward, own_in, onward_in

    ay = ring_pairs(
        lambda i: wa.at[x, i], lambda i, h: wa.at[x, i, h], lambda i: at(x, i, z), y, yp_, ym, yo, 0
    )
    bx = ring_pairs(
        lambda i: wb.at[y, i], lambda i, h: wb.at[y, i, h], lambda i: at(i, y, z), x, xp_, xm, xo, 4
    )
    ax = ring_pairs(
        lambda i: wa.at[i], lambda i, h: wa.at[i, 2 * h : 2 * h + 2], lambda i: at(i, y, z), x, xp_, xm, xo, 8
    )
    by = ring_pairs(
        lambda i: wb.at[i], lambda i, h: wb.at[i, 2 * h : 2 * h + 2], lambda i: at(x, i, z), y, yp_, ym, yo, 12
    )

    def gram(first, last):
        for n in range(first, last):
            i, j = PAIRS[n]
            gsend[n * BLK : (n + 1) * BLK, :] = dot(
                sv[:, i * BLK : (i + 1) * BLK], sv[:, j * BLK : (j + 1) * BLK], TN
            ).astype(BF16)

    def begin(two):
        for pair in zip(*two):
            for copy in pair:
                copy.start()

    def arrived(two):
        for pair in zip(*two):
            for copy in pair:
                copy.wait_recv()

    load_s.wait()
    gram(0, 2)
    for d in (1, 7, 2, 6, 3, 5, 4):
        for a in range(2):
            z_arrival(d, a).wait_recv()
    begin((ay[0], bx[0]))
    gram(2, 5)
    arrived((ay[2], bx[2]))
    begin((ay[1], bx[1]))
    gram(5, 7)
    arrived((ay[3], bx[3]))
    begin((ax[0], by[0]))
    gram(7, 10)

    def piece(ref, k):
        return ref.at[pl.ds(pl.multiple_of(k * PIECE, 16), PIECE), :]

    def gram_out(k):
        to = (ex + k) % N_EX
        return remote(piece(gsend, to), grecv.at[k], g_s.at[k], g_r.at[k], {"ctx": ctx, "ex": to})

    def sum_out(k):
        to = (ex + k) % N_EX
        return remote(piece(cb, ex), piece(cb, ex), c_s.at[k], c_r.at[k], {"ctx": ctx, "ex": to})

    def sum_in(k):
        of = (ex + N_EX - k) % N_EX
        return remote(piece(cb, of), piece(cb, of), c_s.at[k], c_r.at[k], {"ctx": ctx, "ex": of})

    def loop(body):
        def step(k, carry):
            body(k)
            return carry

        lax.fori_loop(1, N_EX, step, 0)

    loop(lambda k: gram_out(k).start())
    arrived((ax[2], by[2]))
    begin((ax[1], by[1]))
    def add_piece(k, total):
        gram_out(k).wait_recv()
        return total + grecv[k].astype(F32)

    own_piece = gsend[pl.ds(pl.multiple_of(ex * PIECE, 16), PIECE), :].astype(F32)
    total = lax.fori_loop(1, N_EX, add_piece, own_piece)
    cb[pl.ds(pl.multiple_of(ex * PIECE, 16), PIECE), :] = total.astype(BF16)
    loop(lambda k: sum_out(k).start())

    load_x.wait()
    load_g.wait()
    for copy in swaps:
        copy.wait_recv()
    arrived((ax[3], by[3]))
    rows = 2 * 128

    def project(n, carry):
        xt, gt = carry
        yy, xx = n // 4, n % 4
        for l in range(2):
            e = (yy * 2 + l) * 4 + xx
            cols = pl.ds(pl.multiple_of(e * 256, 256), 256)
            xt = xt + dot(xa[:, :, cols].reshape(rows, 256), wa[xx, yy, l].reshape(128, 256), NT)
            gt = gt + dot(wb[yy, xx, l].reshape(128, 256), ga[:, :, cols].reshape(rows, 256), NT)
        return xt, gt

    xt, gt = lax.fori_loop(0, 16, project, (jnp.zeros((rows, 128), F32), jnp.zeros((128, rows), F32)))
    xt, gt = xt.astype(BF16), gt.astype(BF16)
    weights = jnp.concatenate([wm[0], wm[1]], axis=1)
    lane = lax.broadcasted_iota(jnp.int32, (32, 128), 1) // 32
    outer = [
        dot((gt.astype(F32) * weights[d : d + 1, :]).astype(BF16), xt, NN) for d in range(DOCS)
    ]
    for h in range(4):
        packed = jnp.zeros((32, 128), F32)
        for d in range(DOCS):
            block = outer[d][h * 32 : (h + 1) * 32, :]
            shift = ((d - h) * 32) % 128
            if shift:
                block = pltpu.roll(block, shift, 1)
            packed = jnp.where(lane == d, block, packed)
        tsend[h] = packed

    def t_out(k):
        to = (zh + k) % 4
        return remote(tsend.at[to], trecv.at[k], t_s.at[k], t_r.at[k], at(x, y, to * 2 + zl))

    for k in (1, 3, 2):
        t_out(k).start()
    spread_lanes = (
        lax.broadcasted_iota(jnp.int32, (128, FEAT), 0) == lax.broadcasted_iota(jnp.int32, (128, FEAT), 1) % 32
    ).astype(F32).astype(BF16)
    keep = lax.broadcasted_iota(jnp.int32, (32, FEAT), 0) == lax.broadcasted_iota(jnp.int32, (32, FEAT), 1) // 32
    grad_sum = tsend[zh]
    for k in (1, 3, 2):
        t_out(k).wait_recv()
        grad_sum = grad_sum + trecv[k]
    high = grad_sum.astype(BF16).astype(F32)
    rest = grad_sum - high
    middle = rest.astype(BF16).astype(F32)
    low = rest - middle
    for d in range(DOCS):
        turned = [pltpu.roll(p, (128 - d * 32) % 128, 1) if d else p for p in (high, middle, low)]
        wide = dot(jnp.concatenate(turned, axis=0).astype(BF16), spread_lanes, NN)
        wide = wide[0:32] + wide[32:64] + wide[64:96]
        row = jnp.sum(jnp.where(keep, wide, 0.0), axis=0, keepdims=True)
        for k in range(8):
            qs[d * 8 + k : d * 8 + k + 1, :] = row[:, k * 128 : (k + 1) * 128]

    def queries_at(e):
        return qg.at[pl.ds(pl.multiple_of(e * 32, 32), 32), :]

    def q_out(k):
        return remote(qs, queries_at(ex), q_s.at[k], q_r.at[k], {"ctx": ctx, "ex": (ex + k) % N_EX})

    def q_in(k):
        of = (ex + N_EX - k) % N_EX
        return remote(qs, queries_at(of), q_s.at[k], q_r.at[k], {"ctx": ctx, "ex": of})

    loop(lambda k: q_out(k).start())
    qg[pl.ds(pl.multiple_of(ex * 32, 32), 32), :] = qs[...]
    loop(lambda k: sum_in(k).wait_recv())
    loop(lambda k: q_in(k).wait_recv())

    def curv(j, i):
        n = PAIRS.index((min(i, j), max(i, j)))
        return cb[n * BLK : (n + 1) * BLK, :], (NN if j <= i else NT)

    diagonal = lax.broadcasted_iota(jnp.int32, (BLK, BLK), 0) == lax.broadcasted_iota(jnp.int32, (BLK, BLK), 1)
    trace = jnp.zeros((1, 1), F32)
    for i in range(NBLK):
        kept = jnp.where(diagonal, curv(i, i)[0].astype(F32), 0.0)
        trace = trace + jnp.sum(jnp.sum(kept, axis=0, keepdims=True), axis=1, keepdims=True)
    mean_diag = trace / STORE / FEAT
    step_size = 1.0 / (spread * (mean_diag + epsilon))

    queries = [
        jnp.concatenate([qg[pl.ds(2 * i + h, 128, stride=8), :] for h in range(2)], axis=1) for i in range(NBLK)
    ]
    iterate = [step_size * q for q in queries]
    for _ in range(STEPS):
        split = []
        for v in iterate:
            top = v.astype(BF16)
            split.append(jnp.concatenate([top, (v - top.astype(F32)).astype(BF16)], axis=0))
        following = []
        for i in range(NBLK):
            both = jnp.zeros((256, BLK), F32)
            for j in range(NBLK):
                block, dims = curv(j, i)
                both = both + dot(split[j], block, dims)
            applied = (both[:128] + both[128:]) / STORE + damping * mean_diag * iterate[i]
            following.append(iterate[i] + step_size * (queries[i] - applied))
        iterate = following
    precond = jnp.concatenate([v.astype(BF16) for v in iterate], axis=1)

    width = 3072 // CHUNKS

    def o_out(n):
        return remote(part.at[n, 1 - core], sib.at[n], o_s.at[n], o_r.at[n], sibling)

    def zo_out(n, k):
        to = (zh + k) % 4
        return remote(zsend.at[n, to], zrecv.at[n, k], zo_s.at[n, k], zo_r.at[n, k], at(x, y, to * 2 + zl))

    def hand_on(n):
        o_out(n).wait_recv()
        for h in range(4):
            zsend[n, h] = (part[n, core, h] + sib[n, h]).astype(BF16)
        for k in (2, 1, 3):
            zo_out(n, k).start()

    for n in range(CHUNKS):
        scores = dot(precond, sv[n * width : (n + 1) * width, :], NT)
        for c in range(8):
            part[n, c % 2, c // 2] = scores[c * 16 : (c + 1) * 16, :]
        o_out(n).start()
        if n:
            hand_on(n - 1)
    hand_on(CHUNKS - 1)
    score_scale = 1.0 / math.sqrt(MODULES * FEAT * LEN / DOCS)
    for n in range(CHUNKS):
        own = part[n, core, zh] + sib[n, zh]
        for k in (1, 3, 2):
            zo_out(n, k).wait_recv()
            own = own + zrecv[n, k].astype(F32)
        out[:, n * width : (n + 1) * width] = own * score_scale

    for d in range(1, 8):
        for a in range(2):
            along_z(d, a).wait_send()
    for copy in swaps:
        copy.wait_send()
    for four in (ay, bx, ax, by):
        for copy in four[0] + four[1]:
            copy.wait_send()
    loop(lambda k: gram_out(k).wait_send())
    loop(lambda k: sum_out(k).wait_send())
    loop(lambda k: q_out(k).wait_send())
    for k in (1, 2, 3):
        t_out(k).wait_send()
        for n in range(CHUNKS):
            zo_out(n, k).wait_send()
    for n in range(CHUNKS):
        o_out(n).wait_send()


def shards(acts, out_grads, projections, segments, valid, stored):
    columns = jnp.transpose(projections, (0, 2, 1))
    vmem = pl.BlockSpec(memory_space=pltpu.VMEM)
    hbm = pl.BlockSpec(memory_space=pl.ANY)
    dma = pltpu.SemaphoreType.DMA
    width = 3072 // CHUNKS
    return pl.pallas_call(
        kernel,
        out_shape=jax.ShapeDtypeStruct((16, 3072), F32),
        in_specs=[vmem, hbm, hbm, vmem, vmem, hbm],
        out_specs=vmem,
        scratch_shapes=[
            pltpu.VMEM((4, 4, 2, 4, 32, 256), BF16),
            pltpu.VMEM((4, 4, 2, 4, 32, 256), BF16),
            pltpu.VMEM((2, 128, 8192), BF16),
            pltpu.VMEM((2, 128, 8192), BF16),
            pltpu.VMEM((3072, FEAT), BF16),
            pltpu.VMEM((2, 8, 128), F32),
            pltpu.VMEM((N_EX * PIECE, BLK), BF16),
            pltpu.VMEM((N_EX, PIECE, BLK), BF16),
            pltpu.VMEM((N_EX * PIECE, BLK), BF16),
            pltpu.VMEM((4, 32, 128), F32),
            pltpu.VMEM((4, 32, 128), F32),
            pltpu.VMEM((32, 128), F32),
            pltpu.VMEM((N_EX * 32, 128), F32),
            pltpu.VMEM((CHUNKS, 2, 4, 16, width), F32),
            pltpu.VMEM((CHUNKS, 4, 16, width), F32),
            pltpu.VMEM((CHUNKS, 4, 16, width), BF16),
            pltpu.VMEM((CHUNKS, 4, 16, width), BF16),
            dma((3,)),
            dma((3,)),
            dma((3,)),
            dma((2, 8)),
            dma((2, 8)),
            dma((16,)),
            dma((16,)),
            dma((N_EX,)),
            dma((N_EX,)),
            dma((N_EX,)),
            dma((N_EX,)),
            dma((4,)),
            dma((4,)),
            dma((N_EX,)),
            dma((N_EX,)),
            dma((CHUNKS,)),
            dma((CHUNKS,)),
            dma((CHUNKS, 4)),
            dma((CHUNKS, 4)),
        ],
        compiler_params=pltpu.CompilerParams(
            collective_id=0, has_side_effects=True, vmem_limit_bytes=50 * 1024 * 1024
        ),
        cost_estimate=pl.CostEstimate(flops=12_000_000_000, bytes_accessed=20_000_000, transcendentals=0),
    )(columns, acts, out_grads, segments, valid, stored)


def solution(mesh):
    in_specs = (
        P("ex", "ctx", None),
        P("ex", "ctx", None),
        P(None, "ex", "ctx"),
        P("ex", "ctx"),
        P("ex", "ctx"),
        P("ex", "ctx"),
    )
    out_specs = P("ctx", "ex")
    return jax.shard_map(shards, mesh=mesh, in_specs=in_specs, out_specs=out_specs, check_vma=False)
```

```python
import math

import jax
import jax.numpy as jnp
from jax import lax
from jax.experimental import pallas as pl
from jax.experimental.pallas import tpu as pltpu
from jax.sharding import PartitionSpec as P

RANK = 32
MODULES = 8
DOCS = 4
STEPS = 4
FEAT = 1024
STORE = 98304
LEN = 1024

damping = 0.1
spread = 1.5
epsilon = 1e-06

MESH = pl.DeviceIdType.MESH
F32 = jnp.float32
BF16 = jnp.bfloat16

N_EX = 32
CHUNKS = 4
BLK = 256
NBLK = FEAT // BLK
PAIRS = [(i, j) for i in range(NBLK) for j in range(i, NBLK)]
HALF = len(PAIRS) * BLK // 2
LONG = HALF // 4
SHORT = LONG // 4

NN = (((1,), (0,)), ((), ()))
NT = (((1,), (1,)), ((), ()))
TN = (((0,), (0,)), ((), ()))


def dot(a, b, dims):
    return lax.dot_general(a, b, dims, preferred_element_type=F32)


def kernel(
    pt, acts, grads, seg, val, stored, out,
    wa, wb, xa, ga, sv, sg, vl, wm, gsend, r1, s1, r2, s2, r3, cb, tsend, trecv, qs, qg, part, sib, zsend, zrecv,
    loc_sem, sib_s, sib_r, z_s, z_r, ring_s, ring_r, rs_s, rs_r, zl_s, zl_r, ag_s, ag_r, t_s, t_r, q_s, q_r,
    o_s, o_r, zo_s, zo_r,
):
    ctx = lax.axis_index("ctx")
    ex = lax.axis_index("ex")
    zh, core = ctx // 2, ctx % 2
    y, zl, x = ex // 8, (ex // 4) % 2, ex % 4
    z = zh * 2 + zl

    def at(xx, yy, zz):
        return {"ctx": (zz // 2) * 2 + core, "ex": (yy * 2 + zz % 2) * 4 + xx}

    sibling = {"ctx": zh * 2 + 1 - core, "ex": ex}

    def remote(src, dst, s, r, device):
        return pltpu.make_async_remote_copy(
            src_ref=src, dst_ref=dst, send_sem=s, recv_sem=r, device_id=device, device_id_type=MESH
        )

    load_s = pltpu.make_async_copy(stored, sv, loc_sem.at[0])
    load_x = pltpu.make_async_copy(acts.at[0], xa.at[0], loc_sem.at[1])
    load_g = pltpu.make_async_copy(grads.at[0], ga.at[0], loc_sem.at[2])
    load_a = pltpu.make_async_copy(pt.at[0], wa.at[x, y, zl, zh], loc_sem.at[3])
    load_b = pltpu.make_async_copy(pt.at[1], wb.at[y, x, zl, zh], loc_sem.at[4])
    load_seg = pltpu.make_async_copy(seg, sg, loc_sem.at[5])
    load_val = pltpu.make_async_copy(val, vl, loc_sem.at[6])
    for copy in (load_seg, load_val, load_a, load_b, load_s, load_x, load_g):
        copy.start()

    barrier = pltpu.get_barrier_semaphore()

    def greet(k, carry):
        pl.semaphore_signal(
            barrier, inc=1, device_id={"ctx": ctx, "ex": (ex + k) % N_EX}, device_id_type=MESH
        )
        return carry

    lax.fori_loop(1, N_EX, greet, 0)
    for dh in range(1, 4):
        for l in range(2):
            pl.semaphore_signal(
                barrier, inc=1, device_id=at(x, y, ((zh + dh) % 4) * 2 + l), device_id_type=MESH
            )
    pl.semaphore_signal(barrier, inc=1, device_id=sibling, device_id_type=MESH)
    load_seg.wait()
    load_val.wait()
    for d in range(8):
        wm[0, d : d + 1, :] = jnp.where((sg[...] == d) & (vl[...] == 1), 1.0, 0.0).astype(F32)
    pl.semaphore_wait(barrier, N_EX - 1 + 7)

    swaps = [
        remote(acts.at[0], xa.at[1], sib_s.at[0], sib_r.at[0], sibling),
        remote(grads.at[0], ga.at[1], sib_s.at[1], sib_r.at[1], sibling),
        remote(wm.at[0], wm.at[1], sib_s.at[2], sib_r.at[2], sibling),
    ]

    def along_z(d, a):
        slot = wa.at[x, y, zl, zh] if a == 0 else wb.at[y, x, zl, zh]
        return remote(pt.at[a], slot, z_s.at[a, d], z_r.at[a, d], at(x, y, (z + d) % 8))

    def z_arrival(d, a):
        zz = (z + 8 - d) % 8
        slot = wa.at[x, y, zz % 2, zz // 2] if a == 0 else wb.at[y, x, zz % 2, zz // 2]
        return remote(pt.at[a], slot, z_s.at[a, d], z_r.at[a, d], at(x, y, zz))

    far = (4, 3, 5, 2, 6, 1, 7)
    for a in range(2):
        for d in far:
            along_z(d, a).start()
    for copy in swaps:
        copy.start()

    xp_, xm, xo = (x + 1) % 4, (x + 3) % 4, (x + 2) % 4
    yp_, ym, yo = (y + 1) % 4, (y + 3) % 4, (y + 2) % 4

    def ring_pairs(block, half, where, me, plus, minus, opposite, first):
        def one(ref, k, device):
            return remote(ref, ref, ring_s.at[first + k], ring_r.at[first + k], device)

        own = [one(block(me), 0, where(plus)), one(block(me), 1, where(minus))]
        onward = [one(half(minus, 0), 2, where(plus)), one(half(plus, 1), 3, where(minus))]
        own_in = [one(block(minus), 0, where(minus)), one(block(plus), 1, where(plus))]
        onward_in = [one(half(opposite, 0), 2, where(minus)), one(half(opposite, 1), 3, where(plus))]
        return own, onward, own_in, onward_in

    ay = ring_pairs(
        lambda i: wa.at[x, i], lambda i, h: wa.at[x, i, h], lambda i: at(x, i, z), y, yp_, ym, yo, 0
    )
    bx = ring_pairs(
        lambda i: wb.at[y, i], lambda i, h: wb.at[y, i, h], lambda i: at(i, y, z), x, xp_, xm, xo, 4
    )
    ax = ring_pairs(
        lambda i: wa.at[i], lambda i, h: wa.at[i, 2 * h : 2 * h + 2], lambda i: at(i, y, z), x, xp_, xm, xo, 8
    )
    by = ring_pairs(
        lambda i: wb.at[i], lambda i, h: wb.at[i, 2 * h : 2 * h + 2], lambda i: at(x, i, z), y, yp_, ym, yo, 12
    )

    def gram(first, last):
        for n in range(first, last):
            i, j = PAIRS[n]
            gsend[n * BLK : (n + 1) * BLK, :] = dot(
                sv[:, i * BLK : (i + 1) * BLK], sv[:, j * BLK : (j + 1) * BLK], TN
            ).astype(BF16)

    def begin(two):
        for pair in zip(*two):
            for copy in pair:
                copy.start()

    def arrived(two):
        for pair in zip(*two):
            for copy in pair:
                copy.wait_recv()

    def along(half, stage, to):
        return at(to, y, z) if half == stage else at(x, to, z)

    def place(half, stage):
        return x if half == stage else y

    def rows_of(ref, first, count):
        return ref.at[pl.ds(pl.multiple_of(first, 16), count), :]

    def gram_out(half, k):
        to = (place(half, 0) + k) % 4
        source = rows_of(gsend, half * HALF + to * LONG, LONG)
        return remote(source, r1.at[half, k], rs_s.at[half, 0, k], rs_r.at[half, 0, k], along(half, 0, to))

    def part_out(half, k):
        to = (place(half, 1) + k) % 4
        source = rows_of(s1.at[half], to * SHORT, SHORT)
        return remote(source, r2.at[half, k], rs_s.at[half, 1, k], rs_r.at[half, 1, k], along(half, 1, to))

    def pair_out(half):
        return remote(s2.at[half], r3.at[half], zl_s.at[half], zl_r.at[half], at(x, y, zh * 2 + 1 - zl))

    def short_block(half, j):
        return rows_of(cb, half * HALF + place(half, 0) * LONG + j * SHORT, SHORT)

    def long_block(half, j):
        return rows_of(cb, half * HALF + j * LONG, LONG)

    def spread_out(half, stage, k, arriving=False):
        me = place(half, stage)
        block = (long_block, short_block)[stage](half, (me + 4 - k) % 4 if arriving else me)
        to = (me + k) % 4
        return remote(block, block, ag_s.at[half, stage, k], ag_r.at[half, stage, k], along(half, stage, to))

    around = (2, 1, 3)
    load_s.wait()
    for half in range(2):
        gram(5 * half, 5 * half + 5)
        for k in around:
            gram_out(half, k).start()
    load_a.wait()
    load_b.wait()
    for a in range(2):
        for d in far:
            z_arrival(d, a).wait_recv()
        for copy in (ay, bx)[a][0]:
            copy.start()
    for half in range(2):
        own = pl.ds(pl.multiple_of(half * HALF + place(half, 0) * LONG, 16), LONG)
        total = gsend[own, :].astype(F32)
        for k in around:
            gram_out(half, k).wait_recv()
            total = total + r1[half, k].astype(F32)
        s1[half] = total
        for k in around:
            part_out(half, k).start()
    arrived((ay[2], bx[2]))
    begin((ay[1], bx[1]))
    arrived((ay[3], bx[3]))
    begin((ax[0], by[0]))
    for half in range(2):
        total = s1[half, pl.ds(pl.multiple_of(place(half, 1) * SHORT, 16), SHORT), :]
        for k in around:
            part_out(half, k).wait_recv()
            total = total + r2[half, k]
        s2[half] = total
        pair_out(half).start()

    load_x.wait()
    load_g.wait()
    for copy in swaps:
        copy.wait_recv()
    rows = 2 * 128

    def project(carry, xx, yy):
        def step(n, carry):
            xt, gt = carry
            for l in range(2):
                cols = pl.ds(pl.multiple_of(((n * 2 + l) * 4 + xx) * 256, 256), 256)
                xt = xt + dot(xa[:, :, cols].reshape(rows, 256), wa[xx, n, l].reshape(128, 256), NT)
                cols = pl.ds(pl.multiple_of(((yy * 2 + l) * 4 + n) * 256, 256), 256)
                gt = gt + dot(wb[yy, n, l].reshape(128, 256), ga[:, :, cols].reshape(rows, 256), NT)
            return xt, gt

        return lax.fori_loop(0, 4, step, carry)

    both = project((jnp.zeros((rows, 128), F32), jnp.zeros((128, rows), F32)), x, y)
    for half in range(2):
        pair_out(half).wait_recv()
        own = pl.ds(pl.multiple_of(half * HALF + place(half, 0) * LONG + place(half, 1) * SHORT, 16), SHORT)
        cb[own, :] = (s2[half] + r3[half]).astype(BF16)
        for k in around:
            spread_out(half, 1, k).start()
    arrived((ax[2], by[2]))
    begin((ax[1], by[1]))
    both = project(both, xm, ym)
    both = project(both, xp_, yp_)
    arrived((ax[3], by[3]))
    for half in range(2):
        for k in around:
            spread_out(half, 1, k, True).wait_recv()
        for k in around:
            spread_out(half, 0, k).start()
    xt, gt = project(both, xo, yo)
    xt, gt = xt.astype(BF16), gt.astype(BF16)
    weights = jnp.concatenate([wm[0], wm[1]], axis=1)
    lane = lax.broadcasted_iota(jnp.int32, (32, 128), 1) // 32
    outer = [
        dot((gt.astype(F32) * weights[d : d + 1, :]).astype(BF16), xt, NN) for d in range(DOCS)
    ]
    for h in range(4):
        packed = jnp.zeros((32, 128), F32)
        for d in range(DOCS):
            block = outer[d][h * 32 : (h + 1) * 32, :]
            shift = ((d - h) * 32) % 128
            if shift:
                block = pltpu.roll(block, shift, 1)
            packed = jnp.where(lane == d, block, packed)
        tsend[h] = packed

    def t_out(k):
        to = (zh + k) % 4
        return remote(tsend.at[to], trecv.at[k], t_s.at[k], t_r.at[k], at(x, y, to * 2 + zl))

    for k in (1, 3, 2):
        t_out(k).start()
    spread_lanes = (
        lax.broadcasted_iota(jnp.int32, (128, FEAT), 0) == lax.broadcasted_iota(jnp.int32, (128, FEAT), 1) % 32
    ).astype(F32).astype(BF16)
    keep = lax.broadcasted_iota(jnp.int32, (32, FEAT), 0) == lax.broadcasted_iota(jnp.int32, (32, FEAT), 1) // 32
    grad_sum = tsend[zh]
    for k in (1, 3, 2):
        t_out(k).wait_recv()
        grad_sum = grad_sum + trecv[k]
    high = grad_sum.astype(BF16).astype(F32)
    rest = grad_sum - high
    middle = rest.astype(BF16).astype(F32)
    low = rest - middle
    for d in range(DOCS):
        turned = [pltpu.roll(p, (128 - d * 32) % 128, 1) if d else p for p in (high, middle, low)]
        wide = dot(jnp.concatenate(turned, axis=0).astype(BF16), spread_lanes, NN)
        wide = wide[0:32] + wide[32:64] + wide[64:96]
        row = jnp.sum(jnp.where(keep, wide, 0.0), axis=0, keepdims=True)
        for k in range(8):
            qs[d * 8 + k : d * 8 + k + 1, :] = row[:, k * 128 : (k + 1) * 128]

    def queries_at(e):
        return qg.at[pl.ds(pl.multiple_of(e * 32, 32), 32), :]

    def q_out(k):
        return remote(qs, queries_at(ex), q_s.at[k], q_r.at[k], {"ctx": ctx, "ex": (ex + k) % N_EX})

    def q_in(k):
        of = (ex + N_EX - k) % N_EX
        return remote(qs, queries_at(of), q_s.at[k], q_r.at[k], {"ctx": ctx, "ex": of})

    def loop(body):
        def step(k, carry):
            body(k)
            return carry

        lax.fori_loop(1, N_EX, step, 0)

    loop(lambda k: q_out(k).start())
    qg[pl.ds(pl.multiple_of(ex * 32, 32), 32), :] = qs[...]
    for half in range(2):
        for k in around:
            spread_out(half, 0, k, True).wait_recv()
    loop(lambda k: q_in(k).wait_recv())

    def curv(j, i):
        n = PAIRS.index((min(i, j), max(i, j)))
        return cb[n * BLK : (n + 1) * BLK, :], (NN if j <= i else NT)

    diagonal = lax.broadcasted_iota(jnp.int32, (BLK, BLK), 0) == lax.broadcasted_iota(jnp.int32, (BLK, BLK), 1)
    trace = jnp.zeros((1, 1), F32)
    for i in range(NBLK):
        kept = jnp.where(diagonal, curv(i, i)[0].astype(F32), 0.0)
        trace = trace + jnp.sum(jnp.sum(kept, axis=0, keepdims=True), axis=1, keepdims=True)
    mean_diag = trace / STORE / FEAT
    step_size = 1.0 / (spread * (mean_diag + epsilon))

    queries = [
        jnp.concatenate([qg[pl.ds(2 * i + h, 128, stride=8), :] for h in range(2)], axis=1) for i in range(NBLK)
    ]
    iterate = [step_size * q for q in queries]
    for _ in range(STEPS):
        split = []
        for v in iterate:
            top = v.astype(BF16)
            split.append(jnp.concatenate([top, (v - top.astype(F32)).astype(BF16)], axis=0))
        following = []
        for i in range(NBLK):
            both = jnp.zeros((256, BLK), F32)
            for j in range(NBLK):
                block, dims = curv(j, i)
                both = both + dot(split[j], block, dims)
            applied = (both[:128] + both[128:]) / STORE + damping * mean_diag * iterate[i]
            following.append(iterate[i] + step_size * (queries[i] - applied))
        iterate = following
    precond = jnp.concatenate([v.astype(BF16) for v in iterate], axis=1)

    width = 3072 // CHUNKS

    def o_out(n):
        return remote(part.at[n, 1 - core], sib.at[n], o_s.at[n], o_r.at[n], sibling)

    def zo_out(n, k):
        to = (zh + k) % 4
        return remote(zsend.at[n, to], zrecv.at[n, k], zo_s.at[n, k], zo_r.at[n, k], at(x, y, to * 2 + zl))

    def hand_on(n):
        o_out(n).wait_recv()
        for h in range(4):
            zsend[n, h] = (part[n, core, h] + sib[n, h]).astype(BF16)
        for k in (2, 1, 3):
            zo_out(n, k).start()

    for n in range(CHUNKS):
        scores = dot(precond, sv[n * width : (n + 1) * width, :], NT)
        for c in range(8):
            part[n, c % 2, c // 2] = scores[c * 16 : (c + 1) * 16, :]
        o_out(n).start()
        if n:
            hand_on(n - 1)
    hand_on(CHUNKS - 1)
    for d in range(1, 8):
        for a in range(2):
            along_z(d, a).wait_send()
    for copy in swaps:
        copy.wait_send()
    for four in (ay, bx, ax, by):
        for copy in four[0] + four[1]:
            copy.wait_send()
    for half in range(2):
        pair_out(half).wait_send()
        for k in around:
            gram_out(half, k).wait_send()
            part_out(half, k).wait_send()
            spread_out(half, 0, k).wait_send()
            spread_out(half, 1, k).wait_send()
    loop(lambda k: q_out(k).wait_send())
    for k in (1, 2, 3):
        t_out(k).wait_send()
    score_scale = 1.0 / math.sqrt(MODULES * FEAT * LEN / DOCS)
    for n in range(CHUNKS):
        own = part[n, core, zh] + sib[n, zh]
        for k in (1, 3, 2):
            zo_out(n, k).wait_recv()
            own = own + zrecv[n, k].astype(F32)
        out[:, n * width : (n + 1) * width] = own * score_scale
    for n in range(CHUNKS):
        o_out(n).wait_send()
        for k in (1, 2, 3):
            zo_out(n, k).wait_send()


def shards(acts, out_grads, projections, segments, valid, stored):
    columns = jnp.transpose(projections, (0, 2, 1))
    vmem = pl.BlockSpec(memory_space=pltpu.VMEM)
    hbm = pl.BlockSpec(memory_space=pltpu.HBM)
    dma = pltpu.SemaphoreType.DMA
    width = 3072 // CHUNKS
    return pl.pallas_call(
        kernel,
        out_shape=jax.ShapeDtypeStruct((16, 3072), F32),
        in_specs=[hbm] * 6,
        out_specs=vmem,
        scratch_shapes=[
            pltpu.VMEM((4, 4, 2, 4, 32, 256), BF16),
            pltpu.VMEM((4, 4, 2, 4, 32, 256), BF16),
            pltpu.VMEM((2, 128, 8192), BF16),
            pltpu.VMEM((2, 128, 8192), BF16),
            pltpu.VMEM((3072, FEAT), BF16),
            pltpu.VMEM((1, 128), jnp.int32),
            pltpu.VMEM((1, 128), jnp.int32),
            pltpu.VMEM((2, 8, 128), F32),
            pltpu.VMEM((2 * HALF, BLK), BF16),
            pltpu.VMEM((2, 4, LONG, BLK), BF16),
            pltpu.VMEM((2, LONG, BLK), F32),
            pltpu.VMEM((2, 4, SHORT, BLK), F32),
            pltpu.VMEM((2, SHORT, BLK), F32),
            pltpu.VMEM((2, SHORT, BLK), F32),
            pltpu.VMEM((2 * HALF, BLK), BF16),
            pltpu.VMEM((4, 32, 128), F32),
            pltpu.VMEM((4, 32, 128), F32),
            pltpu.VMEM((32, 128), F32),
            pltpu.VMEM((N_EX * 32, 128), F32),
            pltpu.VMEM((CHUNKS, 2, 4, 16, width), F32),
            pltpu.VMEM((CHUNKS, 4, 16, width), F32),
            pltpu.VMEM((CHUNKS, 4, 16, width), BF16),
            pltpu.VMEM((CHUNKS, 4, 16, width), BF16),
            dma((7,)),
            dma((3,)),
            dma((3,)),
            dma((2, 8)),
            dma((2, 8)),
            dma((16,)),
            dma((16,)),
            dma((2, 2, 4)),
            dma((2, 2, 4)),
            dma((2,)),
            dma((2,)),
            dma((2, 2, 4)),
            dma((2, 2, 4)),
            dma((4,)),
            dma((4,)),
            dma((N_EX,)),
            dma((N_EX,)),
            dma((CHUNKS,)),
            dma((CHUNKS,)),
            dma((CHUNKS, 4)),
            dma((CHUNKS, 4)),
        ],
        compiler_params=pltpu.CompilerParams(
            collective_id=0, has_side_effects=True, vmem_limit_bytes=60 * 1024 * 1024
        ),
        cost_estimate=pl.CostEstimate(flops=12_000_000_000, bytes_accessed=20_000_000, transcendentals=0),
    )(columns, acts, out_grads, segments, valid, stored)


def solution(mesh):
    in_specs = (
        P("ex", "ctx", None),
        P("ex", "ctx", None),
        P(None, "ex", "ctx"),
        P("ex", "ctx"),
        P("ex", "ctx"),
        P("ex", "ctx"),
    )
    out_specs = P("ctx", "ex")
    return jax.shard_map(shards, mesh=mesh, in_specs=in_specs, out_specs=out_specs, check_vma=False)
```

```python
import math

import jax
import jax.numpy as jnp
from jax import lax
from jax.experimental import pallas as pl
from jax.experimental.pallas import tpu as pltpu
from jax.sharding import PartitionSpec as P

RANK = 32
MODULES = 8
DOCS = 4
STEPS = 4
FEAT = 1024
STORE = 98304
LEN = 1024

damping = 0.1
spread = 1.5
epsilon = 1e-06

MESH = pl.DeviceIdType.MESH
F32 = jnp.float32
BF16 = jnp.bfloat16

N_EX = 32
CHUNKS = 6
BLK = 256
NBLK = FEAT // BLK
PAIRS = [(i, j) for i in range(NBLK) for j in range(i, NBLK)]
HALF = len(PAIRS) * BLK // 2
LONG = HALF // 4
SHORT = LONG // 4

NN = (((1,), (0,)), ((), ()))
NT = (((1,), (1,)), ((), ()))
TN = (((0,), (0,)), ((), ()))


def dot(a, b, dims):
    return lax.dot_general(a, b, dims, preferred_element_type=F32)


def kernel(
    pt, acts, grads, seg, val, stored, out,
    wa, wb, wca, wcb, xa, ga, sv, sg, vl, wm, gsend, r1, s1, s1b, r2, s2, s2b, r3, cb, tsend, trecv, qs, qsb, qg, qf, part, sib, zsend, zrecv,
    loc_sem, sib_s, sib_r, z_s, z_r, ring_s, ring_r, cp_s, cp_r, cz_s, cz_r, rs_s, rs_r, zl_s, zl_r, ag_s, ag_r, t_s, t_r, q_s, q_r,
    o_s, o_r, zo_s, zo_r,
):
    ctx = lax.axis_index("ctx")
    ex = lax.axis_index("ex")
    zh, core = ctx // 2, ctx % 2
    y, zl, x = ex // 8, (ex // 4) % 2, ex % 4
    z = zh * 2 + zl

    def at(xx, yy, zz):
        return {"ctx": (zz // 2) * 2 + core, "ex": (yy * 2 + zz % 2) * 4 + xx}

    sibling = {"ctx": zh * 2 + 1 - core, "ex": ex}

    def remote(src, dst, s, r, device):
        return pltpu.make_async_remote_copy(
            src_ref=src, dst_ref=dst, send_sem=s, recv_sem=r, device_id=device, device_id_type=MESH
        )

    load_s = pltpu.make_async_copy(stored, sv, loc_sem.at[0])
    load_x = pltpu.make_async_copy(acts.at[0], xa.at[0], loc_sem.at[1])
    load_g = pltpu.make_async_copy(grads.at[0], ga.at[0], loc_sem.at[2])
    load_a = pltpu.make_async_copy(pt.at[0, :, 0:128], wa.at[x, y, zl, zh], loc_sem.at[3])
    load_b = pltpu.make_async_copy(pt.at[1, :, 0:128], wb.at[y, x, zl, zh], loc_sem.at[4])
    load_ca = pltpu.make_async_copy(pt.at[0, :, 128:256], wca.at[z, x, y], loc_sem.at[7])
    load_cb = pltpu.make_async_copy(pt.at[1, :, 128:256], wcb.at[z, y, x], loc_sem.at[8])
    load_seg = pltpu.make_async_copy(seg, sg, loc_sem.at[5])
    load_val = pltpu.make_async_copy(val, vl, loc_sem.at[6])
    for copy in (load_seg, load_val, load_a, load_b, load_ca, load_cb, load_s, load_x, load_g):
        copy.start()

    barrier = pltpu.get_barrier_semaphore()

    def greet(k, carry):
        pl.semaphore_signal(
            barrier, inc=1, device_id={"ctx": ctx, "ex": (ex + k) % N_EX}, device_id_type=MESH
        )
        return carry

    lax.fori_loop(1, N_EX, greet, 0)
    for dh in range(1, 4):
        for l in range(2):
            pl.semaphore_signal(
                barrier, inc=1, device_id=at(x, y, ((zh + dh) % 4) * 2 + l), device_id_type=MESH
            )
    pl.semaphore_signal(barrier, inc=1, device_id=sibling, device_id_type=MESH)
    load_seg.wait()
    load_val.wait()
    for d in range(8):
        wm[0, d : d + 1, :] = jnp.where((sg[...] == d) & (vl[...] == 1), 1.0, 0.0).astype(F32)
    pl.semaphore_wait(barrier, N_EX - 1 + 7)

    swaps = [
        remote(acts.at[0], xa.at[1], sib_s.at[0], sib_r.at[0], sibling),
        remote(grads.at[0], ga.at[1], sib_s.at[1], sib_r.at[1], sibling),
        remote(wm.at[0], wm.at[1], sib_s.at[2], sib_r.at[2], sibling),
    ]

    def along_z(d, a):
        slot = wa.at[x, y, zl, zh] if a == 0 else wb.at[y, x, zl, zh]
        return remote(pt.at[a, :, 0:128], slot, z_s.at[a, d], z_r.at[a, d], at(x, y, (z + d) % 8))

    def z_arrival(d, a):
        zz = (z + 8 - d) % 8
        slot = wa.at[x, y, zz % 2, zz // 2] if a == 0 else wb.at[y, x, zz % 2, zz // 2]
        return remote(pt.at[a, :, 0:128], slot, z_s.at[a, d], z_r.at[a, d], at(x, y, zz))

    def plane_out(a, stage, k, arriving=False):
        along_x = (a == 1) == (stage == 0)
        me = x if along_x else y
        i = (me + 4 - k) % 4 if arriving else me
        to = (me + k) % 4
        if stage == 0:
            block = wca.at[z, x, i] if a == 0 else wcb.at[z, y, i]
            source = pt.at[a, :, 128:256]
        else:
            block = wca.at[z, i] if a == 0 else wcb.at[z, i]
            source = block
        return remote(
            source, block, cp_s.at[a, stage, k], cp_r.at[a, stage, k], at(to, y, z) if along_x else at(x, to, z)
        )

    def round_z(t, arriving=False):
        copies = []
        for way in (0, 1):
            sign = 1 if way == 0 else 7
            for a in range(2):
                if t == 4 and a != way:
                    continue
                zz = (z + (8 - sign) * (t if arriving else t - 1)) % 8
                block = wca.at[zz] if a == 0 else wcb.at[zz]
                copies.append(remote(block, block, cz_s.at[a, way, t], cz_r.at[a, way, t], at(x, y, (z + sign) % 8)))
        return copies

    far = (4, 3, 5, 2, 6, 1, 7)
    for a in range(2):
        for d in far:
            along_z(d, a).start()
    around = (2, 1, 3)
    for k in around:
        for a in range(2):
            plane_out(a, 0, k).start()
    for copy in swaps:
        copy.start()

    xp_, xm, xo = (x + 1) % 4, (x + 3) % 4, (x + 2) % 4
    yp_, ym, yo = (y + 1) % 4, (y + 3) % 4, (y + 2) % 4

    def ring_pairs(block, half, where, me, plus, minus, opposite, first):
        def one(ref, k, device):
            return remote(ref, ref, ring_s.at[first + k], ring_r.at[first + k], device)

        own = [one(block(me), 0, where(plus)), one(block(me), 1, where(minus))]
        onward = [one(half(minus, 0), 2, where(plus)), one(half(plus, 1), 3, where(minus))]
        own_in = [one(block(minus), 0, where(minus)), one(block(plus), 1, where(plus))]
        onward_in = [one(half(opposite, 0), 2, where(minus)), one(half(opposite, 1), 3, where(plus))]
        return own, onward, own_in, onward_in

    ay = ring_pairs(
        lambda i: wa.at[x, i], lambda i, h: wa.at[x, i, h], lambda i: at(x, i, z), y, yp_, ym, yo, 0
    )
    bx = ring_pairs(
        lambda i: wb.at[y, i], lambda i, h: wb.at[y, i, h], lambda i: at(i, y, z), x, xp_, xm, xo, 4
    )
    ax = ring_pairs(
        lambda i: wa.at[i], lambda i, h: wa.at[i, 2 * h : 2 * h + 2], lambda i: at(i, y, z), x, xp_, xm, xo, 8
    )
    by = ring_pairs(
        lambda i: wb.at[i], lambda i, h: wb.at[i, 2 * h : 2 * h + 2], lambda i: at(x, i, z), y, yp_, ym, yo, 12
    )

    def gram(first, last):
        for n in range(first, last):
            i, j = PAIRS[n]
            gsend[n * BLK : (n + 1) * BLK, :] = dot(
                sv[:, i * BLK : (i + 1) * BLK], sv[:, j * BLK : (j + 1) * BLK], TN
            ).astype(BF16)

    def begin(two):
        for pair in zip(*two):
            for copy in pair:
                copy.start()

    def arrived(two):
        for pair in zip(*two):
            for copy in pair:
                copy.wait_recv()

    def along(half, stage, to):
        return at(to, y, z) if half == stage else at(x, to, z)

    def place(half, stage):
        return x if half == stage else y

    def rows_of(ref, first, count):
        return ref.at[pl.ds(pl.multiple_of(first, 16), count), :]

    def gram_out(half, k):
        to = (place(half, 0) + k) % 4
        source = rows_of(gsend, half * HALF + to * LONG, LONG)
        return remote(source, r1.at[half, k], rs_s.at[half, 0, k], rs_r.at[half, 0, k], along(half, 0, to))

    def part_out(half, k):
        to = (place(half, 1) + k) % 4
        source = rows_of(s1b.at[half], to * SHORT, SHORT)
        return remote(source, r2.at[half, k], rs_s.at[half, 1, k], rs_r.at[half, 1, k], along(half, 1, to))

    def pair_out(half):
        return remote(s2b.at[half], r3.at[half], zl_s.at[half], zl_r.at[half], at(x, y, zh * 2 + 1 - zl))

    def short_block(half, j):
        return rows_of(cb, half * HALF + place(half, 0) * LONG + j * SHORT, SHORT)

    def long_block(half, j):
        return rows_of(cb, half * HALF + j * LONG, LONG)

    def spread_out(half, stage, k, arriving=False):
        me = place(half, stage)
        block = (long_block, short_block)[stage](half, (me + 4 - k) % 4 if arriving else me)
        to = (me + k) % 4
        return remote(block, block, ag_s.at[half, stage, k], ag_r.at[half, stage, k], along(half, stage, to))

    load_s.wait()
    for half in range(2):
        gram(5 * half, 5 * half + 5)
        for k in around:
            gram_out(half, k).start()
        if half == 0:
            load_ca.wait()
            load_cb.wait()
            for a in range(2):
                for k in around:
                    plane_out(a, 0, k, True).wait_recv()
                for k in around:
                    plane_out(a, 1, k).start()
    load_a.wait()
    load_b.wait()
    for a in range(2):
        for d in far:
            z_arrival(d, a).wait_recv()
        for copy in (ay, bx)[a][0]:
            copy.start()
    for a in range(2):
        for k in around:
            plane_out(a, 1, k, True).wait_recv()
    for copy in round_z(1):
        copy.start()
    for half in range(2):
        own = pl.ds(pl.multiple_of(half * HALF + place(half, 0) * LONG, 16), LONG)
        total = gsend[own, :].astype(F32)
        for k in around:
            gram_out(half, k).wait_recv()
            total = total + r1[half, k].astype(F32)
        s1[half] = total
        s1b[half] = total.astype(BF16)
        for k in around:
            part_out(half, k).start()
    def onward_z(t):
        for copy in round_z(t, True):
            copy.wait_recv()
        if t < 4:
            for copy in round_z(t + 1):
                copy.start()

    arrived((ay[2], bx[2]))
    begin((ay[1], bx[1]))
    arrived((ay[3], bx[3]))
    begin((ax[0], by[0]))
    onward_z(1)
    for half in range(2):
        total = s1[half, pl.ds(pl.multiple_of(place(half, 1) * SHORT, 16), SHORT), :]
        for k in around:
            part_out(half, k).wait_recv()
            total = total + r2[half, k].astype(F32)
        s2[half] = total
        s2b[half] = total.astype(BF16)
        pair_out(half).start()

    load_x.wait()
    load_g.wait()
    for copy in swaps:
        copy.wait_recv()
    rows = 2 * 128

    def lanes(ref, first, second):
        return jnp.concatenate(
            [ref[:, :, pl.ds(pl.multiple_of(c, 128), 128)].reshape(rows, 128) for c in (first, second)], axis=1
        )

    def beside(first, second):
        return jnp.concatenate([first, second], axis=1)

    def project(carry, xx, yy):
        def step(n, carry):
            xt, gt = carry
            c = (n * 8 + xx) * 256
            block = beside(wa[xx, n, 0].reshape(128, 128), wa[xx, n, 1].reshape(128, 128))
            xt = xt + dot(lanes(xa, c, c + 1024), block, NT)
            c = (yy * 8 + n) * 256
            block = beside(wb[yy, n, 0].reshape(128, 128), wb[yy, n, 1].reshape(128, 128))
            gt = gt + dot(block, lanes(ga, c, c + 1024), NT)
            return xt, gt

        return lax.fori_loop(0, 4, step, carry)

    def project_planes(carry, l):
        def of(ref, i, j):
            return jnp.concatenate([ref[2 * h + l, i, j] for h in range(4)], axis=0)

        def step(n, carry):
            xt, gt = carry
            for p in range(2):
                c = (n * 8 + l * 4 + 2 * p) * 256 + 128
                xt = xt + dot(lanes(xa, c, c + 256), beside(of(wca, 2 * p, n), of(wca, 2 * p + 1, n)), NT)
                gt = gt + dot(beside(of(wcb, n, 2 * p), of(wcb, n, 2 * p + 1)), lanes(ga, c, c + 256), NT)
            return xt, gt

        return lax.fori_loop(0, 4, step, carry)

    both = project((jnp.zeros((rows, 128), F32), jnp.zeros((128, rows), F32)), x, y)
    onward_z(2)
    for half in range(2):
        pair_out(half).wait_recv()
        own = pl.ds(pl.multiple_of(half * HALF + place(half, 0) * LONG + place(half, 1) * SHORT, 16), SHORT)
        cb[own, :] = (s2[half] + r3[half].astype(F32)).astype(BF16)
        for k in around:
            spread_out(half, 1, k).start()
    arrived((ax[2], by[2]))
    begin((ax[1], by[1]))
    both = project(both, xm, ym)
    both = project(both, xp_, yp_)
    onward_z(3)
    both = project_planes(both, 1 - zl)
    arrived((ax[3], by[3]))
    for half in range(2):
        for k in around:
            spread_out(half, 1, k, True).wait_recv()
        for k in around:
            spread_out(half, 0, k).start()
    both = project(both, xo, yo)
    onward_z(4)
    xt, gt = project_planes(both, zl)
    xt, gt = xt.astype(BF16), gt.astype(BF16)
    weights = jnp.concatenate([wm[0], wm[1]], axis=1)
    lane = lax.broadcasted_iota(jnp.int32, (32, 128), 1) // 32
    outer = [
        dot((gt.astype(F32) * weights[d : d + 1, :]).astype(BF16), xt, NN) for d in range(DOCS)
    ]
    for h in range(4):
        packed = jnp.zeros((32, 128), F32)
        for d in range(DOCS):
            block = outer[d][h * 32 : (h + 1) * 32, :]
            shift = ((d - h) * 32) % 128
            if shift:
                block = pltpu.roll(block, shift, 1)
            packed = jnp.where(lane == d, block, packed)
        tsend[h] = packed

    def t_out(k):
        to = (zh + k) % 4
        return remote(tsend.at[to], trecv.at[k], t_s.at[k], t_r.at[k], at(x, y, to * 2 + zl))

    for k in (1, 3, 2):
        t_out(k).start()
    spread_lanes = (
        lax.broadcasted_iota(jnp.int32, (128, FEAT), 0) == lax.broadcasted_iota(jnp.int32, (128, FEAT), 1) % 32
    ).astype(F32).astype(BF16)
    keep = lax.broadcasted_iota(jnp.int32, (32, FEAT), 0) == lax.broadcasted_iota(jnp.int32, (32, FEAT), 1) // 32
    grad_sum = tsend[zh]
    for k in (1, 3, 2):
        t_out(k).wait_recv()
        grad_sum = grad_sum + trecv[k]
    high = grad_sum.astype(BF16).astype(F32)
    rest = grad_sum - high
    middle = rest.astype(BF16).astype(F32)
    low = rest - middle
    for d in range(DOCS):
        turned = [pltpu.roll(p, (128 - d * 32) % 128, 1) if d else p for p in (high, middle, low)]
        wide = dot(jnp.concatenate(turned, axis=0).astype(BF16), spread_lanes, NN)
        wide = wide[0:32] + wide[32:64] + wide[64:96]
        row = jnp.sum(jnp.where(keep, wide, 0.0), axis=0, keepdims=True)
        for k in range(8):
            qs[d * 8 + k : d * 8 + k + 1, :] = row[:, k * 128 : (k + 1) * 128]

    def queries_at(e):
        return qg.at[pl.ds(pl.multiple_of(e * 32, 32), 32), :]

    def q_out(k):
        return remote(qsb, queries_at(ex), q_s.at[k], q_r.at[k], {"ctx": ctx, "ex": (ex + k) % N_EX})

    def q_in(k):
        of = (ex + N_EX - k) % N_EX
        return remote(qsb, queries_at(of), q_s.at[k], q_r.at[k], {"ctx": ctx, "ex": of})

    def loop(body):
        def step(k, carry):
            body(k)
            return carry

        lax.fori_loop(1, N_EX, step, 0)

    qsb[...] = qs[...].astype(BF16)
    loop(lambda k: q_out(k).start())
    qg[pl.ds(pl.multiple_of(ex * 32, 32), 32), :] = qsb[...]
    for half in range(2):
        for k in around:
            spread_out(half, 0, k, True).wait_recv()
    loop(lambda k: q_in(k).wait_recv())
    qf[...] = qg[...].astype(F32)

    def curv(j, i):
        n = PAIRS.index((min(i, j), max(i, j)))
        return cb[n * BLK : (n + 1) * BLK, :], (NN if j <= i else NT)

    diagonal = lax.broadcasted_iota(jnp.int32, (BLK, BLK), 0) == lax.broadcasted_iota(jnp.int32, (BLK, BLK), 1)
    trace = jnp.zeros((1, 1), F32)
    for i in range(NBLK):
        kept = jnp.where(diagonal, curv(i, i)[0].astype(F32), 0.0)
        trace = trace + jnp.sum(jnp.sum(kept, axis=0, keepdims=True), axis=1, keepdims=True)
    mean_diag = trace / STORE / FEAT
    step_size = 1.0 / (spread * (mean_diag + epsilon))

    queries = [
        jnp.concatenate([qf[pl.ds(2 * i + h, 128, stride=8), :] for h in range(2)], axis=1) for i in range(NBLK)
    ]
    iterate = [step_size * q for q in queries]
    for _ in range(STEPS):
        split = []
        for v in iterate:
            top = v.astype(BF16)
            split.append(jnp.concatenate([top, (v - top.astype(F32)).astype(BF16)], axis=0))
        following = []
        for i in range(NBLK):
            both = jnp.zeros((256, BLK), F32)
            for j in range(NBLK):
                block, dims = curv(j, i)
                both = both + dot(split[j], block, dims)
            applied = (both[:128] + both[128:]) / STORE + damping * mean_diag * iterate[i]
            following.append(iterate[i] + step_size * (queries[i] - applied))
        iterate = following
    precond = jnp.concatenate([v.astype(BF16) for v in iterate], axis=1)

    width = 3072 // CHUNKS

    def o_out(n):
        return remote(part.at[n, 1 - core], sib.at[n], o_s.at[n], o_r.at[n], sibling)

    def zo_out(n, k):
        to = (zh + k) % 4
        return remote(zsend.at[n, to], zrecv.at[n, k], zo_s.at[n, k], zo_r.at[n, k], at(x, y, to * 2 + zl))

    def hand_on(n):
        o_out(n).wait_recv()
        for h in range(4):
            zsend[n, h] = (part[n, core, h] + sib[n, h]).astype(BF16)
        for k in (2, 1, 3):
            zo_out(n, k).start()

    for n in range(CHUNKS):
        scores = dot(precond, sv[n * width : (n + 1) * width, :], NT)
        for c in range(8):
            part[n, c % 2, c // 2] = scores[c * 16 : (c + 1) * 16, :]
        o_out(n).start()
        if n:
            hand_on(n - 1)
    hand_on(CHUNKS - 1)
    for d in range(1, 8):
        for a in range(2):
            along_z(d, a).wait_send()
    for copy in swaps:
        copy.wait_send()
    for t in range(1, 5):
        for copy in round_z(t):
            copy.wait_send()
    for a in range(2):
        for k in around:
            plane_out(a, 0, k).wait_send()
            plane_out(a, 1, k).wait_send()
    for four in (ay, bx, ax, by):
        for copy in four[0] + four[1]:
            copy.wait_send()
    for half in range(2):
        pair_out(half).wait_send()
        for k in around:
            gram_out(half, k).wait_send()
            part_out(half, k).wait_send()
            spread_out(half, 0, k).wait_send()
            spread_out(half, 1, k).wait_send()
    loop(lambda k: q_out(k).wait_send())
    for k in (1, 2, 3):
        t_out(k).wait_send()
    score_scale = 1.0 / math.sqrt(MODULES * FEAT * LEN / DOCS)
    for n in range(CHUNKS):
        own = part[n, core, zh] + sib[n, zh]
        for k in (1, 3, 2):
            zo_out(n, k).wait_recv()
            own = own + zrecv[n, k].astype(F32)
        out[:, n * width : (n + 1) * width] = own * score_scale
    for n in range(CHUNKS):
        o_out(n).wait_send()
        for k in (1, 2, 3):
            zo_out(n, k).wait_send()


def shards(acts, out_grads, projections, segments, valid, stored):
    columns = jnp.transpose(projections, (0, 2, 1))
    vmem = pl.BlockSpec(memory_space=pltpu.VMEM)
    hbm = pl.BlockSpec(memory_space=pltpu.HBM)
    dma = pltpu.SemaphoreType.DMA
    width = 3072 // CHUNKS
    return pl.pallas_call(
        kernel,
        out_shape=jax.ShapeDtypeStruct((16, 3072), F32),
        in_specs=[hbm] * 6,
        out_specs=vmem,
        scratch_shapes=[
            pltpu.VMEM((4, 4, 2, 4, 32, 128), BF16),
            pltpu.VMEM((4, 4, 2, 4, 32, 128), BF16),
            pltpu.VMEM((8, 4, 4, 32, 128), BF16),
            pltpu.VMEM((8, 4, 4, 32, 128), BF16),
            pltpu.VMEM((2, 128, 8192), BF16),
            pltpu.VMEM((2, 128, 8192), BF16),
            pltpu.VMEM((3072, FEAT), BF16),
            pltpu.VMEM((1, 128), jnp.int32),
            pltpu.VMEM((1, 128), jnp.int32),
            pltpu.VMEM((2, 8, 128), F32),
            pltpu.VMEM((2 * HALF, BLK), BF16),
            pltpu.VMEM((2, 4, LONG, BLK), BF16),
            pltpu.VMEM((2, LONG, BLK), F32),
            pltpu.VMEM((2, LONG, BLK), BF16),
            pltpu.VMEM((2, 4, SHORT, BLK), BF16),
            pltpu.VMEM((2, SHORT, BLK), F32),
            pltpu.VMEM((2, SHORT, BLK), BF16),
            pltpu.VMEM((2, SHORT, BLK), BF16),
            pltpu.VMEM((2 * HALF, BLK), BF16),
            pltpu.VMEM((4, 32, 128), F32),
            pltpu.VMEM((4, 32, 128), F32),
            pltpu.VMEM((32, 128), F32),
            pltpu.VMEM((32, 128), BF16),
            pltpu.VMEM((N_EX * 32, 128), BF16),
            pltpu.VMEM((N_EX * 32, 128), F32),
            pltpu.VMEM((CHUNKS, 2, 4, 16, width), F32),
            pltpu.VMEM((CHUNKS, 4, 16, width), F32),
            pltpu.VMEM((CHUNKS, 4, 16, width), BF16),
            pltpu.VMEM((CHUNKS, 4, 16, width), BF16),
            dma((9,)),
            dma((3,)),
            dma((3,)),
            dma((2, 8)),
            dma((2, 8)),
            dma((16,)),
            dma((16,)),
            dma((2, 2, 4)),
            dma((2, 2, 4)),
            dma((2, 2, 5)),
            dma((2, 2, 5)),
            dma((2, 2, 4)),
            dma((2, 2, 4)),
            dma((2,)),
            dma((2,)),
            dma((2, 2, 4)),
            dma((2, 2, 4)),
            dma((4,)),
            dma((4,)),
            dma((N_EX,)),
            dma((N_EX,)),
            dma((CHUNKS,)),
            dma((CHUNKS,)),
            dma((CHUNKS, 4)),
            dma((CHUNKS, 4)),
        ],
        compiler_params=pltpu.CompilerParams(
            collective_id=0, has_side_effects=True, vmem_limit_bytes=60 * 1024 * 1024
        ),
        cost_estimate=pl.CostEstimate(flops=12_000_000_000, bytes_accessed=20_000_000, transcendentals=0),
    )(columns, acts, out_grads, segments, valid, stored)


def solution(mesh):
    in_specs = (
        P("ex", "ctx", None),
        P("ex", "ctx", None),
        P(None, "ex", "ctx"),
        P("ex", "ctx"),
        P("ex", "ctx"),
        P("ex", "ctx"),
    )
    out_specs = P("ctx", "ex")
    return jax.shard_map(shards, mesh=mesh, in_specs=in_specs, out_specs=out_specs, check_vma=False)
```

```python
import math

import jax
import jax.numpy as jnp
from jax import lax
from jax.experimental import pallas as pl
from jax.experimental.pallas import tpu as pltpu
from jax.sharding import PartitionSpec as P

RANK = 32
MODULES = 8
DOCS = 4
STEPS = 4
FEAT = 1024
STORE = 98304
LEN = 1024

damping = 0.1
spread = 1.5
epsilon = 1e-06

MESH = pl.DeviceIdType.MESH
F32 = jnp.float32
BF16 = jnp.bfloat16

N_EX = 32
CHUNKS = 8
BLK = 256
NBLK = FEAT // BLK
PAIRS = [(i, j) for i in range(NBLK) for j in range(i, NBLK)]
HALF = len(PAIRS) * BLK // 2
LONG = HALF // 4
SHORT = LONG // 4

NN = (((1,), (0,)), ((), ()))
NT = (((1,), (1,)), ((), ()))
TN = (((0,), (0,)), ((), ()))


def dot(a, b, dims):
    return lax.dot_general(a, b, dims, preferred_element_type=F32)


def kernel(
    pt, acts, grads, seg, val, stored, out,
    wa, wb, wca, wcb, xa, ga, sv, sg, vl, wm, gsend, r1, s1, s1b, r2, s2, s2b, r3, cb, tsend, trecv, qs, qsb, qg, qf, part, sib, zsend, zrecv,
    loc_sem, sib_s, sib_r, z_s, z_r, ring_s, ring_r, cp_s, cp_r, cz_s, cz_r, rs_s, rs_r, zl_s, zl_r, ag_s, ag_r, t_s, t_r, q_s, q_r,
    o_s, o_r, zo_s, zo_r,
):
    ctx = lax.axis_index("ctx")
    ex = lax.axis_index("ex")
    zh, core = ctx // 2, ctx % 2
    y, zl, x = ex // 8, (ex // 4) % 2, ex % 4
    z = zh * 2 + zl

    def at(xx, yy, zz):
        return {"ctx": (zz // 2) * 2 + core, "ex": (yy * 2 + zz % 2) * 4 + xx}

    sibling = {"ctx": zh * 2 + 1 - core, "ex": ex}

    def remote(src, dst, s, r, device):
        return pltpu.make_async_remote_copy(
            src_ref=src, dst_ref=dst, send_sem=s, recv_sem=r, device_id=device, device_id_type=MESH
        )

    load_s = pltpu.make_async_copy(stored, sv, loc_sem.at[0])
    load_x = pltpu.make_async_copy(acts.at[0], xa.at[0], loc_sem.at[1])
    load_g = pltpu.make_async_copy(grads.at[0], ga.at[0], loc_sem.at[2])
    load_a = pltpu.make_async_copy(pt.at[0, :, 0:128], wa.at[x, y, zl, zh], loc_sem.at[3])
    load_b = pltpu.make_async_copy(pt.at[1, :, 0:128], wb.at[y, x, zl, zh], loc_sem.at[4])
    load_ca = pltpu.make_async_copy(pt.at[0, :, 128:256], wca.at[z, x, y], loc_sem.at[7])
    load_cb = pltpu.make_async_copy(pt.at[1, :, 128:256], wcb.at[z, y, x], loc_sem.at[8])
    load_seg = pltpu.make_async_copy(seg, sg, loc_sem.at[5])
    load_val = pltpu.make_async_copy(val, vl, loc_sem.at[6])
    for copy in (load_seg, load_val, load_a, load_b, load_ca, load_cb, load_s, load_x, load_g):
        copy.start()

    barrier = pltpu.get_barrier_semaphore()

    def greet(k, carry):
        pl.semaphore_signal(
            barrier, inc=1, device_id={"ctx": ctx, "ex": (ex + k) % N_EX}, device_id_type=MESH
        )
        return carry

    lax.fori_loop(1, N_EX, greet, 0)
    for dh in range(1, 4):
        for l in range(2):
            pl.semaphore_signal(
                barrier, inc=1, device_id=at(x, y, ((zh + dh) % 4) * 2 + l), device_id_type=MESH
            )
    pl.semaphore_signal(barrier, inc=1, device_id=sibling, device_id_type=MESH)
    load_seg.wait()
    load_val.wait()
    for d in range(8):
        wm[0, d : d + 1, :] = jnp.where((sg[...] == d) & (vl[...] == 1), 1.0, 0.0).astype(F32)
    pl.semaphore_wait(barrier, N_EX - 1 + 7)

    swaps = [
        remote(acts.at[0], xa.at[1], sib_s.at[0], sib_r.at[0], sibling),
        remote(grads.at[0], ga.at[1], sib_s.at[1], sib_r.at[1], sibling),
        remote(wm.at[0], wm.at[1], sib_s.at[2], sib_r.at[2], sibling),
    ]

    def along_z(d, a):
        slot = wa.at[x, y, zl, zh] if a == 0 else wb.at[y, x, zl, zh]
        return remote(pt.at[a, :, 0:128], slot, z_s.at[a, d], z_r.at[a, d], at(x, y, (z + d) % 8))

    def z_arrival(d, a):
        zz = (z + 8 - d) % 8
        slot = wa.at[x, y, zz % 2, zz // 2] if a == 0 else wb.at[y, x, zz % 2, zz // 2]
        return remote(pt.at[a, :, 0:128], slot, z_s.at[a, d], z_r.at[a, d], at(x, y, zz))

    def plane_out(a, stage, k, arriving=False):
        along_x = (a == 1) == (stage == 0)
        me = x if along_x else y
        i = (me + 4 - k) % 4 if arriving else me
        to = (me + k) % 4
        if stage == 0:
            block = wca.at[z, x, i] if a == 0 else wcb.at[z, y, i]
            source = pt.at[a, :, 128:256]
        else:
            block = wca.at[z, i] if a == 0 else wcb.at[z, i]
            source = block
        return remote(
            source, block, cp_s.at[a, stage, k], cp_r.at[a, stage, k], at(to, y, z) if along_x else at(x, to, z)
        )

    def round_z(t, arriving=False):
        copies = []
        for a in range(2):
            for way in (0, 1):
                sign = 1 if way == 0 else 7
                if t == 4 and a != way:
                    continue
                zz = (z + (8 - sign) * (t if arriving else t - 1)) % 8
                block = wca.at[zz] if a == 0 else wcb.at[zz]
                copies.append(remote(block, block, cz_s.at[a, way, t], cz_r.at[a, way, t], at(x, y, (z + sign) % 8)))
        return copies

    far = (4, 3, 5, 2, 6, 1, 7)
    for a in range(2):
        for d in far:
            along_z(d, a).start()
    around = (2, 1, 3)
    for k in around:
        for a in range(2):
            plane_out(a, 0, k).start()
    for copy in swaps:
        copy.start()

    xp_, xm, xo = (x + 1) % 4, (x + 3) % 4, (x + 2) % 4
    yp_, ym, yo = (y + 1) % 4, (y + 3) % 4, (y + 2) % 4

    def ring_pairs(block, half, where, me, plus, minus, opposite, first):
        def one(ref, k, device):
            return remote(ref, ref, ring_s.at[first + k], ring_r.at[first + k], device)

        own = [one(block(me), 0, where(plus)), one(block(me), 1, where(minus))]
        onward = [one(half(minus, 0), 2, where(plus)), one(half(plus, 1), 3, where(minus))]
        own_in = [one(block(minus), 0, where(minus)), one(block(plus), 1, where(plus))]
        onward_in = [one(half(opposite, 0), 2, where(minus)), one(half(opposite, 1), 3, where(plus))]
        return own, onward, own_in, onward_in

    ay = ring_pairs(
        lambda i: wa.at[x, i], lambda i, h: wa.at[x, i, h], lambda i: at(x, i, z), y, yp_, ym, yo, 0
    )
    bx = ring_pairs(
        lambda i: wb.at[y, i], lambda i, h: wb.at[y, i, h], lambda i: at(i, y, z), x, xp_, xm, xo, 4
    )
    ax = ring_pairs(
        lambda i: wa.at[i], lambda i, h: wa.at[i, 2 * h : 2 * h + 2], lambda i: at(i, y, z), x, xp_, xm, xo, 8
    )
    by = ring_pairs(
        lambda i: wb.at[i], lambda i, h: wb.at[i, 2 * h : 2 * h + 2], lambda i: at(x, i, z), y, yp_, ym, yo, 12
    )

    def gram(first, last):
        for n in range(first, last):
            i, j = PAIRS[n]
            gsend[n * BLK : (n + 1) * BLK, :] = dot(
                sv[:, i * BLK : (i + 1) * BLK], sv[:, j * BLK : (j + 1) * BLK], TN
            ).astype(BF16)

    def begin(two):
        for pair in zip(*two):
            for copy in pair:
                copy.start()

    def arrived(two):
        for pair in zip(*two):
            for copy in pair:
                copy.wait_recv()

    def along(half, stage, to):
        return at(to, y, z) if half == stage else at(x, to, z)

    def place(half, stage):
        return x if half == stage else y

    def rows_of(ref, first, count):
        return ref.at[pl.ds(pl.multiple_of(first, 16), count), :]

    def gram_out(half, k):
        to = (place(half, 0) + k) % 4
        source = rows_of(gsend, half * HALF + to * LONG, LONG)
        return remote(source, r1.at[half, k], rs_s.at[half, 0, k], rs_r.at[half, 0, k], along(half, 0, to))

    def part_out(half, k):
        to = (place(half, 1) + k) % 4
        source = rows_of(s1b.at[half], to * SHORT, SHORT)
        return remote(source, r2.at[half, k], rs_s.at[half, 1, k], rs_r.at[half, 1, k], along(half, 1, to))

    def pair_out(half):
        return remote(s2b.at[half], r3.at[half], zl_s.at[half], zl_r.at[half], at(x, y, zh * 2 + 1 - zl))

    def short_block(half, j):
        return rows_of(cb, half * HALF + place(half, 0) * LONG + j * SHORT, SHORT)

    def long_block(half, j):
        return rows_of(cb, half * HALF + j * LONG, LONG)

    def spread_out(half, stage, k, arriving=False):
        me = place(half, stage)
        block = (long_block, short_block)[stage](half, (me + 4 - k) % 4 if arriving else me)
        to = (me + k) % 4
        return remote(block, block, ag_s.at[half, stage, k], ag_r.at[half, stage, k], along(half, stage, to))

    load_s.wait()
    for half in range(2):
        gram(5 * half, 5 * half + 5)
        for k in around:
            gram_out(half, k).start()
        if half == 0:
            load_ca.wait()
            load_cb.wait()
            for a in range(2):
                for k in around:
                    plane_out(a, 0, k, True).wait_recv()
                for k in around:
                    plane_out(a, 1, k).start()
    load_a.wait()
    load_b.wait()
    for a in range(2):
        for d in far:
            z_arrival(d, a).wait_recv()
        for copy in (ay, bx)[a][0]:
            copy.start()
    for a in range(2):
        for k in around:
            plane_out(a, 1, k, True).wait_recv()
    for copy in round_z(1):
        copy.start()
    for half in range(2):
        own = pl.ds(pl.multiple_of(half * HALF + place(half, 0) * LONG, 16), LONG)
        total = gsend[own, :].astype(F32)
        for k in around:
            gram_out(half, k).wait_recv()
            total = total + r1[half, k].astype(F32)
        s1[half] = total
        s1b[half] = total.astype(BF16)
        for k in around:
            part_out(half, k).start()
    def onward_z(t):
        coming, going = round_z(t, True), round_z(t + 1) if t < 4 else []
        for a in range(2):
            for copy in coming[a * len(coming) // 2 : (a + 1) * len(coming) // 2]:
                copy.wait_recv()
            for copy in going[a * len(going) // 2 : (a + 1) * len(going) // 2]:
                copy.start()

    arrived((ay[2], bx[2]))
    begin((ay[1], bx[1]))
    arrived((ay[3], bx[3]))
    begin((ax[0], by[0]))
    onward_z(1)
    for half in range(2):
        total = s1[half, pl.ds(pl.multiple_of(place(half, 1) * SHORT, 16), SHORT), :]
        for k in around:
            part_out(half, k).wait_recv()
            total = total + r2[half, k].astype(F32)
        s2[half] = total
        s2b[half] = total.astype(BF16)
        pair_out(half).start()

    load_x.wait()
    load_g.wait()
    for copy in swaps:
        copy.wait_recv()
    rows = 2 * 128

    def lanes(ref, first, second):
        return jnp.concatenate(
            [ref[:, :, pl.ds(pl.multiple_of(c, 128), 128)].reshape(rows, 128) for c in (first, second)], axis=1
        )

    def beside(first, second):
        return jnp.concatenate([first, second], axis=1)

    def project(carry, xx, yy):
        def step(n, carry):
            xt, gt = carry
            c = (n * 8 + xx) * 256
            block = beside(wa[xx, n, 0].reshape(128, 128), wa[xx, n, 1].reshape(128, 128))
            xt = xt + dot(lanes(xa, c, c + 1024), block, NT)
            c = (yy * 8 + n) * 256
            block = beside(wb[yy, n, 0].reshape(128, 128), wb[yy, n, 1].reshape(128, 128))
            gt = gt + dot(block, lanes(ga, c, c + 1024), NT)
            return xt, gt

        return lax.fori_loop(0, 4, step, carry)

    def project_planes(carry, l):
        def of(ref, i, j):
            return jnp.concatenate([ref[2 * h + l, i, j] for h in range(4)], axis=0)

        def step(n, carry):
            xt, gt = carry
            for p in range(2):
                c = (n * 8 + l * 4 + 2 * p) * 256 + 128
                xt = xt + dot(lanes(xa, c, c + 256), beside(of(wca, 2 * p, n), of(wca, 2 * p + 1, n)), NT)
                gt = gt + dot(beside(of(wcb, n, 2 * p), of(wcb, n, 2 * p + 1)), lanes(ga, c, c + 256), NT)
            return xt, gt

        return lax.fori_loop(0, 4, step, carry)

    both = project((jnp.zeros((rows, 128), F32), jnp.zeros((128, rows), F32)), x, y)
    onward_z(2)
    for half in range(2):
        pair_out(half).wait_recv()
        own = pl.ds(pl.multiple_of(half * HALF + place(half, 0) * LONG + place(half, 1) * SHORT, 16), SHORT)
        cb[own, :] = (s2[half] + r3[half].astype(F32)).astype(BF16)
        for k in around:
            spread_out(half, 1, k).start()
    arrived((ax[2], by[2]))
    begin((ax[1], by[1]))
    both = project(both, xm, ym)
    both = project(both, xp_, yp_)
    onward_z(3)
    both = project_planes(both, 1 - zl)
    arrived((ax[3], by[3]))
    for half in range(2):
        for k in around:
            spread_out(half, 1, k, True).wait_recv()
        for k in around:
            spread_out(half, 0, k).start()
    both = project(both, xo, yo)
    onward_z(4)
    xt, gt = project_planes(both, zl)
    xt, gt = xt.astype(BF16), gt.astype(BF16)
    weights = jnp.concatenate([wm[0], wm[1]], axis=1)
    lane = lax.broadcasted_iota(jnp.int32, (32, 128), 1) // 32
    outer = [
        dot((gt.astype(F32) * weights[d : d + 1, :]).astype(BF16), xt, NN) for d in range(DOCS)
    ]
    for h in range(4):
        packed = jnp.zeros((32, 128), F32)
        for d in range(DOCS):
            block = outer[d][h * 32 : (h + 1) * 32, :]
            shift = ((d - h) * 32) % 128
            if shift:
                block = pltpu.roll(block, shift, 1)
            packed = jnp.where(lane == d, block, packed)
        tsend[h] = packed

    def t_out(k):
        to = (zh + k) % 4
        return remote(tsend.at[to], trecv.at[k], t_s.at[k], t_r.at[k], at(x, y, to * 2 + zl))

    for k in (1, 3, 2):
        t_out(k).start()
    spread_lanes = (
        lax.broadcasted_iota(jnp.int32, (128, FEAT), 0) == lax.broadcasted_iota(jnp.int32, (128, FEAT), 1) % 32
    ).astype(F32).astype(BF16)
    keep = lax.broadcasted_iota(jnp.int32, (32, FEAT), 0) == lax.broadcasted_iota(jnp.int32, (32, FEAT), 1) // 32
    grad_sum = tsend[zh]
    for k in (1, 3, 2):
        t_out(k).wait_recv()
        grad_sum = grad_sum + trecv[k]
    high = grad_sum.astype(BF16).astype(F32)
    rest = grad_sum - high
    middle = rest.astype(BF16).astype(F32)
    low = rest - middle
    for d in range(DOCS):
        turned = [pltpu.roll(p, (128 - d * 32) % 128, 1) if d else p for p in (high, middle, low)]
        wide = dot(jnp.concatenate(turned, axis=0).astype(BF16), spread_lanes, NN)
        wide = wide[0:32] + wide[32:64] + wide[64:96]
        row = jnp.sum(jnp.where(keep, wide, 0.0), axis=0, keepdims=True)
        for k in range(8):
            qs[d * 8 + k : d * 8 + k + 1, :] = row[:, k * 128 : (k + 1) * 128]

    def queries_at(e):
        return qg.at[pl.ds(pl.multiple_of(e * 32, 32), 32), :]

    def q_out(k):
        return remote(qsb, queries_at(ex), q_s.at[k], q_r.at[k], {"ctx": ctx, "ex": (ex + k) % N_EX})

    def q_in(k):
        of = (ex + N_EX - k) % N_EX
        return remote(qsb, queries_at(of), q_s.at[k], q_r.at[k], {"ctx": ctx, "ex": of})

    def loop(body):
        def step(k, carry):
            body(k)
            return carry

        lax.fori_loop(1, N_EX, step, 0)

    qsb[...] = qs[...].astype(BF16)
    loop(lambda k: q_out(k).start())
    qg[pl.ds(pl.multiple_of(ex * 32, 32), 32), :] = qsb[...]
    for half in range(2):
        for k in around:
            spread_out(half, 0, k, True).wait_recv()
    loop(lambda k: q_in(k).wait_recv())
    qf[...] = qg[...].astype(F32)

    def curv(j, i):
        n = PAIRS.index((min(i, j), max(i, j)))
        return cb[n * BLK : (n + 1) * BLK, :], (NN if j <= i else NT)

    diagonal = lax.broadcasted_iota(jnp.int32, (BLK, BLK), 0) == lax.broadcasted_iota(jnp.int32, (BLK, BLK), 1)
    trace = jnp.zeros((1, 1), F32)
    for i in range(NBLK):
        kept = jnp.where(diagonal, curv(i, i)[0].astype(F32), 0.0)
        trace = trace + jnp.sum(jnp.sum(kept, axis=0, keepdims=True), axis=1, keepdims=True)
    mean_diag = trace / STORE / FEAT
    step_size = 1.0 / (spread * (mean_diag + epsilon))

    queries = [
        jnp.concatenate([qf[pl.ds(2 * i + h, 128, stride=8), :] for h in range(2)], axis=1) for i in range(NBLK)
    ]
    iterate = [step_size * q for q in queries]
    for _ in range(STEPS):
        split = []
        for v in iterate:
            top = v.astype(BF16)
            split.append(jnp.concatenate([top, (v - top.astype(F32)).astype(BF16)], axis=0))
        following = []
        for i in range(NBLK):
            both = jnp.zeros((256, BLK), F32)
            for j in range(NBLK):
                block, dims = curv(j, i)
                both = both + dot(split[j], block, dims)
            applied = (both[:128] + both[128:]) / STORE + damping * mean_diag * iterate[i]
            following.append(iterate[i] + step_size * (queries[i] - applied))
        iterate = following
    precond = jnp.concatenate([v.astype(BF16) for v in iterate], axis=1)

    width = 3072 // CHUNKS

    def o_out(n):
        return remote(part.at[n, 1 - core], sib.at[n], o_s.at[n], o_r.at[n], sibling)

    def zo_out(n, k):
        to = (zh + k) % 4
        return remote(zsend.at[n, to], zrecv.at[n, k], zo_s.at[n, k], zo_r.at[n, k], at(x, y, to * 2 + zl))

    def hand_on(n):
        o_out(n).wait_recv()
        for h in range(4):
            zsend[n, h] = (part[n, core, h] + sib[n, h]).astype(BF16)
        for k in (2, 1, 3):
            zo_out(n, k).start()

    for n in range(CHUNKS):
        scores = dot(precond, sv[n * width : (n + 1) * width, :], NT)
        for c in range(8):
            part[n, c % 2, c // 2] = scores[c * 16 : (c + 1) * 16, :]
        o_out(n).start()
        if n:
            hand_on(n - 1)
    hand_on(CHUNKS - 1)
    for d in range(1, 8):
        for a in range(2):
            along_z(d, a).wait_send()
    for copy in swaps:
        copy.wait_send()
    for t in range(1, 5):
        for copy in round_z(t):
            copy.wait_send()
    for a in range(2):
        for k in around:
            plane_out(a, 0, k).wait_send()
            plane_out(a, 1, k).wait_send()
    for four in (ay, bx, ax, by):
        for copy in four[0] + four[1]:
            copy.wait_send()
    for half in range(2):
        pair_out(half).wait_send()
        for k in around:
            gram_out(half, k).wait_send()
            part_out(half, k).wait_send()
            spread_out(half, 0, k).wait_send()
            spread_out(half, 1, k).wait_send()
    loop(lambda k: q_out(k).wait_send())
    for k in (1, 2, 3):
        t_out(k).wait_send()
    score_scale = 1.0 / math.sqrt(MODULES * FEAT * LEN / DOCS)
    for n in range(CHUNKS):
        own = part[n, core, zh] + sib[n, zh]
        for k in (1, 3, 2):
            zo_out(n, k).wait_recv()
            own = own + zrecv[n, k].astype(F32)
        out[:, n * width : (n + 1) * width] = own * score_scale
    for n in range(CHUNKS):
        o_out(n).wait_send()
        for k in (1, 2, 3):
            zo_out(n, k).wait_send()


def shards(acts, out_grads, projections, segments, valid, stored):
    columns = jnp.transpose(projections, (0, 2, 1))
    vmem = pl.BlockSpec(memory_space=pltpu.VMEM)
    hbm = pl.BlockSpec(memory_space=pltpu.HBM)
    dma = pltpu.SemaphoreType.DMA
    width = 3072 // CHUNKS
    return pl.pallas_call(
        kernel,
        out_shape=jax.ShapeDtypeStruct((16, 3072), F32),
        in_specs=[hbm] * 6,
        out_specs=vmem,
        scratch_shapes=[
            pltpu.VMEM((4, 4, 2, 4, 32, 128), BF16),
            pltpu.VMEM((4, 4, 2, 4, 32, 128), BF16),
            pltpu.VMEM((8, 4, 4, 32, 128), BF16),
            pltpu.VMEM((8, 4, 4, 32, 128), BF16),
            pltpu.VMEM((2, 128, 8192), BF16),
            pltpu.VMEM((2, 128, 8192), BF16),
            pltpu.VMEM((3072, FEAT), BF16),
            pltpu.VMEM((1, 128), jnp.int32),
            pltpu.VMEM((1, 128), jnp.int32),
            pltpu.VMEM((2, 8, 128), F32),
            pltpu.VMEM((2 * HALF, BLK), BF16),
            pltpu.VMEM((2, 4, LONG, BLK), BF16),
            pltpu.VMEM((2, LONG, BLK), F32),
            pltpu.VMEM((2, LONG, BLK), BF16),
            pltpu.VMEM((2, 4, SHORT, BLK), BF16),
            pltpu.VMEM((2, SHORT, BLK), F32),
            pltpu.VMEM((2, SHORT, BLK), BF16),
            pltpu.VMEM((2, SHORT, BLK), BF16),
            pltpu.VMEM((2 * HALF, BLK), BF16),
            pltpu.VMEM((4, 32, 128), F32),
            pltpu.VMEM((4, 32, 128), F32),
            pltpu.VMEM((32, 128), F32),
            pltpu.VMEM((32, 128), BF16),
            pltpu.VMEM((N_EX * 32, 128), BF16),
            pltpu.VMEM((N_EX * 32, 128), F32),
            pltpu.VMEM((CHUNKS, 2, 4, 16, width), F32),
            pltpu.VMEM((CHUNKS, 4, 16, width), F32),
            pltpu.VMEM((CHUNKS, 4, 16, width), BF16),
            pltpu.VMEM((CHUNKS, 4, 16, width), BF16),
            dma((9,)),
            dma((3,)),
            dma((3,)),
            dma((2, 8)),
            dma((2, 8)),
            dma((16,)),
            dma((16,)),
            dma((2, 2, 4)),
            dma((2, 2, 4)),
            dma((2, 2, 5)),
            dma((2, 2, 5)),
            dma((2, 2, 4)),
            dma((2, 2, 4)),
            dma((2,)),
            dma((2,)),
            dma((2, 2, 4)),
            dma((2, 2, 4)),
            dma((4,)),
            dma((4,)),
            dma((N_EX,)),
            dma((N_EX,)),
            dma((CHUNKS,)),
            dma((CHUNKS,)),
            dma((CHUNKS, 4)),
            dma((CHUNKS, 4)),
        ],
        compiler_params=pltpu.CompilerParams(
            collective_id=0, has_side_effects=True, vmem_limit_bytes=60 * 1024 * 1024
        ),
        cost_estimate=pl.CostEstimate(flops=12_000_000_000, bytes_accessed=20_000_000, transcendentals=0),
    )(columns, acts, out_grads, segments, valid, stored)


def solution(mesh):
    in_specs = (
        P("ex", "ctx", None),
        P("ex", "ctx", None),
        P(None, "ex", "ctx"),
        P("ex", "ctx"),
        P("ex", "ctx"),
        P("ex", "ctx"),
    )
    out_specs = P("ctx", "ex")
    return jax.shard_map(shards, mesh=mesh, in_specs=in_specs, out_specs=out_specs, check_vma=False)
```
